256 devices in a mesh: user: 8 (over y, core), cand: 32 (over z, x).
Axes of the slice: x: 4, y: 4, z: 8, core: 2. Of those that a mesh axis runs over, the one named last changes fastest.
Arguments:
- cand_tokens: bfloat16 [8, 24576, 1024], P('user', 'cand'), may hold values from -6 to 6
- hist_keys: bfloat16 [8, 2048, 1024], P('user', 'cand'), may hold values from -6 to 6
- hist_values: bfloat16 [8, 2048, 1024], P('user', 'cand'), may hold values from -6 to 6
- hist_len: int32 [8], P('user'), may hold values from 512 to 2048, as said below
- cand_count: int32 [8], P('user'), may hold values from 3072 to 24576, as said below
- impressions: int32 [8, 24576], P('user', 'cand'), may hold values from 0 to 24575, each once within a row
- w_proj: bfloat16 [1024, 2048], P(None, 'user'), may hold values from -0.1875 to 0.1875
- w_out: bfloat16 [1024, 1024], replicated, may hold values from -0.1875 to 0.1875
- score_w: float32 [1024], replicated, may hold values from -0.1875 to 0.1875
Outputs:
- layer_out: bfloat16 [8, 24576, 1024], P('user', 'cand')
- ranked: float32 [8, 24576], P('user', 'cand')
The draws below stay inside these ranges and needn't reach their ends.
Inputs may be any that keep to these rules, and one draw needn't show every extreme that they name: `hist_len`: some user has exactly 2048. `cand_count`: some user has exactly 24576. `impressions`: each row is a permutation of the slots.
All inputs are finite; a program needn't handle non-finite values.
Results may differ from the reference program's by a relative error of at most 0.0054.
Values may be sent and summed in bfloat16 or wider, within the bound.
No kernel may reach another device: no remote copies, remote signals or barrier semaphores. Data moves between devices by JAX's collectives and lax.ppermute only.
A program may use at most 128 MiB of HBM per device.

```python
import jax
import jax.numpy as jnp
from jax import lax

D = 1024
HEADS = 8
HIST = 2048
USERS = 8
CANDS = 24576


def draw_hist_len(key, part):
    key = jax.random.fold_in(key, 11)
    first, second = jax.random.split(key)
    drawn = jax.random.randint(first, (USERS,), HIST // 4, HIST + 1)
    chosen = jax.random.randint(second, (), 0, USERS)
    return jnp.where(jnp.arange(USERS) == chosen, HIST, drawn).astype(jnp.int32)


def draw_cand_count(key, part):
    key = jax.random.fold_in(key, 23)
    first, second = jax.random.split(key)
    drawn = jax.random.randint(first, (USERS,), CANDS // 8, CANDS + 1)
    chosen = jax.random.randint(second, (), 0, USERS)
    return jnp.where(jnp.arange(USERS) == chosen, CANDS, drawn).astype(jnp.int32)


def shard_levels(key, shape, cuts, least, largest):
    factor_of, own = 1.0, jax.random.fold_in(key, 6)
    for position, parts in cuts:
        heights = jnp.exp(jax.random.uniform(jax.random.fold_in(own, position), (parts,), jnp.float32, least / len(cuts), largest / len(cuts)))
        factor_of = factor_of * jnp.repeat(heights, shape[position] // parts).reshape([-1 if axis == position else 1 for axis in range(len(shape))])
    return factor_of


def gaussian(own_key, dims, deviation, bound, cuts=(), kind=jnp.bfloat16):
    array = deviation * jax.random.normal(own_key, dims, jnp.float32)
    if cuts:
        array = array * shard_levels(own_key, dims, cuts, -0.22, 0.18)
    return jnp.clip(array, -bound, bound).astype(kind)


def setup_inputs(seed: int = 0) -> dict:
    splits = jax.random.split(jax.random.key(seed), 10)
    cand_tokens = gaussian(splits[0], (USERS, CANDS, D), 1.0, 6.0, ((0, 8), (1, 32)))
    hist_keys = gaussian(splits[1], (USERS, HIST, D), 1.0, 6.0, ((0, 8), (1, 32)))
    hist_values = gaussian(splits[2], (USERS, HIST, D), 1.0, 6.0, ((0, 8), (1, 32)))
    hist_len = draw_hist_len(jax.random.fold_in(splits[9], 71), 0)
    cand_count = draw_cand_count(jax.random.fold_in(splits[9], 71), 0)
    impressions = jax.vmap(lambda own: jax.random.permutation(own, CANDS))(jax.random.split(splits[5], USERS)).reshape((USERS, CANDS)).astype(jnp.int32)
    w_proj = gaussian(splits[6], (D, 2 * D), D ** -0.5, 0.1875, ((1, 8),))
    w_out = gaussian(splits[7], (D, D), D ** -0.5, 0.1875)
    score_w = gaussian(splits[8], (D,), D ** -0.5, 0.1875, (), jnp.float32)
    return {"cand_tokens": cand_tokens, "hist_keys": hist_keys, "hist_values": hist_values, "hist_len": hist_len, "cand_count": cand_count, "impressions": impressions, "w_proj": w_proj, "w_out": w_out, "score_w": score_w}


eps = 1e-05

def layer_norm(values):
    mean = lax.optimization_barrier(jnp.mean(values, axis=-1, keepdims=True))
    centered = values - mean
    var = lax.optimization_barrier(jnp.mean(centered * centered, axis=-1, keepdims=True))
    return centered * lax.rsqrt(var + eps)

def reference(cand_tokens, hist_keys, hist_values, hist_len, cand_count, impressions, w_proj, w_out, score_w):
    head_size = D // HEADS
    factor = float(head_size) ** (-0.5)

    def one_user(packed):
        tokens, keys, values, length, count, order = packed
        inputs = tokens.astype(jnp.float32)
        normed = layer_norm(inputs).astype(jnp.bfloat16)
        proj = jax.nn.silu(jnp.dot(normed, w_proj, preferred_element_type=jnp.float32)).astype(jnp.bfloat16)
        gate = proj[:, :D]
        query = proj[:, D:]
        query3 = query.reshape(CANDS, HEADS, head_size).transpose(1, 0, 2)
        keys3 = keys.reshape(HIST, HEADS, head_size).transpose(1, 0, 2)
        values3 = values.reshape(HIST, HEADS, head_size).transpose(1, 0, 2)
        valid = jnp.arange(HIST, dtype=jnp.int32) < length
        length_f = length.astype(jnp.float32)

        def per_head(trio):
            q_head, k_head, v_head = trio
            scores = jnp.einsum('rd,nd->rn', q_head.astype(jnp.float32), k_head.astype(jnp.float32))
            weight = jnp.where(valid[None, :], jax.nn.silu(factor * scores) / length_f, 0.0).astype(jnp.bfloat16)
            return jnp.dot(weight, v_head, preferred_element_type=jnp.float32)
        attn = lax.map(per_head, (query3, keys3, values3))
        attn = attn.transpose(1, 0, 2).reshape(CANDS, D)
        gated = (layer_norm(attn) * gate.astype(jnp.float32)).astype(jnp.bfloat16)
        outputs = inputs + jnp.dot(gated, w_out, preferred_element_type=jnp.float32)
        live = jnp.arange(CANDS, dtype=jnp.int32) < count
        score = jnp.where(live, jnp.dot(outputs, score_w, precision=lax.Precision.HIGHEST), 0.0)
        ranked_row = jnp.take(score, order, axis=0)
        return (outputs.astype(jnp.bfloat16), ranked_row)
    layer_out, ranked = lax.map(one_user, (cand_tokens, hist_keys, hist_values, hist_len, cand_count, impressions))
    return (layer_out, ranked)
```

```python
import functools

import jax
import jax.numpy as jnp
from jax import lax
from jax.experimental import pallas as pl
from jax.experimental.pallas import tpu as pltpu
from jax.sharding import Mesh
from jax.sharding import PartitionSpec as P

HEADS = 8
eps = 1e-05
VMEM_LIMIT = 48 * 2**20


def params():
    return pltpu.CompilerParams(vmem_limit_bytes=VMEM_LIMIT)


def layer_norm(values):
    mean = jnp.mean(values, axis=-1, keepdims=True)
    centered = values - mean
    var = jnp.mean(centered * centered, axis=-1, keepdims=True)
    return centered * lax.rsqrt(var + eps)


def shifted(size, step):
    return [(i, (i + step) % size) for i in range(size)]


def project_kernel(order_ref, tokens_ref, w_ref, out_ref, normed):
    @pl.when(pl.program_id(0) == 0)
    def _():
        normed[...] = layer_norm(tokens_ref[...].astype(jnp.float32)).astype(jnp.bfloat16)

    x = jnp.dot(normed[...], w_ref[0], preferred_element_type=jnp.float32)
    half = 0.5 * x
    out_ref[...] = (half + half * jnp.tanh(half)).astype(jnp.bfloat16)


def project(tokens, blocks, order):
    rows, width = tokens.shape
    count, _, columns = blocks.shape
    return pl.pallas_call(
        project_kernel,
        grid_spec=pltpu.PrefetchScalarGridSpec(
            num_scalar_prefetch=1,
            grid=(count,),
            in_specs=[
                pl.BlockSpec((rows, width), lambda j, o: (0, 0)),
                pl.BlockSpec((1, width, columns), lambda j, o: (o[j], 0, 0)),
            ],
            out_specs=pl.BlockSpec((rows, columns), lambda j, o: (0, j)),
            scratch_shapes=[pltpu.VMEM((rows, width), jnp.bfloat16)],
        ),
        out_shape=jax.ShapeDtypeStruct((rows, count * columns), jnp.bfloat16),
        compiler_params=params(),
        cost_estimate=pl.CostEstimate(
            flops=2 * rows * width * count * columns, bytes_accessed=9 * 2**20, transcendentals=rows * count * columns
        ),
    )(order, tokens, blocks)


def attend_kernel(q_ref, k_ref, v_ref, scale_ref, out_ref, *, factor, tile):
    head = q_ref.shape[1]
    k = k_ref[...].reshape(-1, head)
    v = v_ref[...].reshape(-1, head)
    for r in range(0, q_ref.shape[0], tile):
        s = lax.dot_general(
            q_ref[r : r + tile, :], k, (((1,), (1,)), ((), ())), preferred_element_type=jnp.float32
        )
        w = (s * jnp.tanh(s * (0.5 * factor)) + s).astype(jnp.bfloat16)
        out_ref[r : r + tile, :] = jnp.dot(w, v, preferred_element_type=jnp.float32) * scale_ref[0]


def attend(proj, history, scale, width):
    rows = proj.shape[0]
    parts, both, _ = history.shape
    own = both // 2
    head = width // HEADS
    return pl.pallas_call(
        functools.partial(attend_kernel, factor=float(head) ** -0.5, tile=256),
        grid=(HEADS,),
        in_specs=[
            pl.BlockSpec((rows, head), lambda h: (0, HEADS + h)),
            pl.BlockSpec((parts, own, head), lambda h: (0, 0, h)),
            pl.BlockSpec((parts, own, head), lambda h: (0, 1, h)),
            pl.BlockSpec(memory_space=pltpu.SMEM),
        ],
        out_specs=pl.BlockSpec((rows, head), lambda h: (0, h)),
        out_shape=jax.ShapeDtypeStruct((rows, width), jnp.float32),
        compiler_params=params(),
        cost_estimate=pl.CostEstimate(
            flops=8 * rows * parts * own * width, bytes_accessed=12 * 2**20, transcendentals=rows * parts * own * HEADS
        ),
    )(proj, history, history, scale)


def gate_kernel(attn_ref, gate_ref, tokens_ref, w_ref, sw_ref, live_ref, gated_ref, score_ref, ws):
    @pl.when(pl.program_id(0) == 0)
    def _():
        ws[...] = lax.dot_general(
            sw_ref[...],
            w_ref[...].astype(jnp.float32),
            (((1,), (1,)), ((), ())),
            precision=lax.Precision.HIGHEST,
            preferred_element_type=jnp.float32,
        )

    gated = (layer_norm(attn_ref[...]) * gate_ref[...].astype(jnp.float32)).astype(jnp.bfloat16)
    gated_ref[...] = gated
    total = gated.astype(jnp.float32) * ws[...] + tokens_ref[...].astype(jnp.float32) * sw_ref[...]
    score = jnp.sum(total, axis=-1)
    first = pl.program_id(0) * score.shape[0]
    slots = first + lax.broadcasted_iota(jnp.int32, (1, score.shape[0]), 1)
    score_ref[...] = jnp.where(slots < live_ref[0], score.reshape(1, -1), 0.0)


def gate_and_score(attn, proj, tokens, w_out, score_w, live, tile=256):
    rows, width = tokens.shape
    return pl.pallas_call(
        gate_kernel,
        grid=(rows // tile,),
        in_specs=[
            pl.BlockSpec((tile, width), lambda i: (i, 0)),
            pl.BlockSpec((tile, width), lambda i: (i, 0)),
            pl.BlockSpec((tile, width), lambda i: (i, 0)),
            pl.BlockSpec((width, width), lambda i: (0, 0)),
            pl.BlockSpec((1, width), lambda i: (0, 0)),
            pl.BlockSpec(memory_space=pltpu.SMEM),
        ],
        out_specs=[pl.BlockSpec((tile, width), lambda i: (i, 0)), pl.BlockSpec((1, tile), lambda i: (0, i))],
        out_shape=[
            jax.ShapeDtypeStruct((rows, width), jnp.bfloat16),
            jax.ShapeDtypeStruct((1, rows), jnp.float32),
        ],
        scratch_shapes=[pltpu.VMEM((1, width), jnp.float32)],
        compiler_params=params(),
    )(attn, proj, tokens, w_out, score_w, live)


def out_kernel(gated_ref, w_ref, tokens_ref, out_ref):
    y = tokens_ref[...].astype(jnp.float32) + jnp.dot(gated_ref[...], w_ref[...], preferred_element_type=jnp.float32)
    out_ref[...] = y.astype(jnp.bfloat16)


def project_out(gated, w_out, tokens, tile=256):
    rows, width = tokens.shape
    return pl.pallas_call(
        out_kernel,
        grid=(rows // tile,),
        in_specs=[
            pl.BlockSpec((tile, width), lambda i: (i, 0)),
            pl.BlockSpec((width, width), lambda i: (0, 0)),
            pl.BlockSpec((tile, width), lambda i: (i, 0)),
        ],
        out_specs=pl.BlockSpec((tile, width), lambda i: (i, 0)),
        out_shape=jax.ShapeDtypeStruct((rows, width), jnp.bfloat16),
        compiler_params=params(),
        cost_estimate=pl.CostEstimate(flops=2 * rows * width * width, bytes_accessed=7 * 2**20, transcendentals=0),
    )(gated, w_out, tokens)


def pick_kernel(index_ref, table_ref, out_ref):
    index = index_ref[...]
    count = index.shape[0]
    height, lanes = table_ref.shape
    onehot = (lax.broadcasted_iota(jnp.int32, (count, height), 1) == index // lanes).astype(jnp.bfloat16)
    rest = table_ref[...]
    rows = jnp.zeros((count, lanes), jnp.float32)
    for _ in range(3):
        part = rest.astype(jnp.bfloat16)
        rows += jnp.dot(onehot, part, preferred_element_type=jnp.float32)
        rest = rest - part.astype(jnp.float32)
    mine = lax.broadcasted_iota(jnp.int32, (count, lanes), 1) == index % lanes
    out_ref[...] = jnp.sum(jnp.where(mine, rows, 0.0), axis=-1).reshape(1, -1)


def pick(index, table):
    count = index.shape[0]
    return pl.pallas_call(
        pick_kernel,
        out_shape=jax.ShapeDtypeStruct((1, count), jnp.float32),
        compiler_params=params(),
    )(index.reshape(count, 1), table.reshape(-1, 128))


def on_device(
    cand_tokens, hist_keys, hist_values, hist_len, cand_count, impressions, w_proj, w_out, score_w
):
    tokens = cand_tokens[0]
    rows, width = tokens.shape
    own = hist_keys.shape[1]
    cand = lax.axis_index(("z", "x"))
    y, core = lax.axis_index("y"), lax.axis_index("core")
    many_y, many_core = lax.axis_size("y"), lax.axis_size("core")
    parts = lax.axis_size(("z", "x"))

    position = cand * own + jnp.arange(own, dtype=jnp.int32)
    keys = jnp.where((position < hist_len[0])[:, None], hist_keys[0], jnp.zeros((), jnp.bfloat16))
    mine = jnp.concatenate([keys, hist_values[0]], axis=0)
    history = lax.all_gather(mine, ("z", "x"), axis=0, tiled=False)

    blocks = [w_proj] + [lax.ppermute(w_proj, "y", shifted(many_y, step)) for step in range(1, many_y)]
    blocks = [each for block in blocks for each in (block, lax.ppermute(block, "core", [(0, 1), (1, 0)]))]
    user = jnp.arange(many_y * many_core, dtype=jnp.int32)
    order = ((y - user // many_core) % many_y) * many_core + (user % many_core != core).astype(jnp.int32)
    proj = project(tokens, jnp.stack(blocks), order.astype(jnp.int32))

    scale = 0.5 * float(width // HEADS) ** -0.5 / hist_len.astype(jnp.float32)
    attn = attend(proj, history, scale, width)
    live = cand_count - cand * rows
    gated, score = gate_and_score(attn, proj, tokens, w_out, score_w[None, :], live)
    sent = jnp.broadcast_to(score[:, None, :], (parts, 1, rows))
    every = lax.all_to_all(sent, ("z", "x"), split_axis=0, concat_axis=0, tiled=True)
    layer_out = project_out(gated, w_out, tokens)
    ranked = pick(impressions[0], every)
    return (layer_out[None], ranked)


def solution(mesh):
    split = Mesh(mesh.devices.reshape(4, 2, 8, 4), ("y", "core", "z", "x"))
    users, cands = ("y", "core"), ("z", "x")
    return jax.shard_map(
        on_device,
        mesh=split,
        in_specs=(
            P(users, cands, None),
            P(users, cands, None),
            P(users, cands, None),
            P(users),
            P(users),
            P(users, cands),
            P(None, users),
            P(),
            P(),
        ),
        out_specs=(P(users, cands, None), P(users, cands)),
        check_vma=False,
    )
```

```python
import functools

import jax
import jax.numpy as jnp
from jax import lax
from jax.experimental import pallas as pl
from jax.experimental.pallas import tpu as pltpu
from jax.sharding import Mesh
from jax.sharding import PartitionSpec as P

HEADS = 8
eps = 1e-05
VMEM_LIMIT = 58 * 2**20


def params():
    return pltpu.CompilerParams(vmem_limit_bytes=VMEM_LIMIT)


def layer_norm(values):
    mean = jnp.mean(values, axis=-1, keepdims=True)
    centered = values - mean
    var = jnp.mean(centered * centered, axis=-1, keepdims=True)
    return centered * lax.rsqrt(var + eps)


def shifted(size, step):
    return [(i, (i + step) % size) for i in range(size)]


def prepare_kernel(tokens_ref, w_ref, sw_ref, normed_ref, ws_ref):
    normed_ref[...] = layer_norm(tokens_ref[...].astype(jnp.float32)).astype(jnp.bfloat16)
    ws_ref[...] = lax.dot_general(
        sw_ref[...],
        w_ref[...].astype(jnp.float32),
        (((1,), (1,)), ((), ())),
        precision=lax.Precision.HIGHEST,
        preferred_element_type=jnp.float32,
    )


def prepare(tokens, w_out, score_w, steps=4):
    rows, width = tokens.shape
    tile, part = rows // steps, width // steps
    return pl.pallas_call(
        prepare_kernel,
        grid=(steps,),
        in_specs=[
            pl.BlockSpec((tile, width), lambda i: (i, 0)),
            pl.BlockSpec((part, width), lambda i: (i, 0)),
            pl.BlockSpec((1, width), lambda i: (0, 0)),
        ],
        out_specs=[pl.BlockSpec((tile, width), lambda i: (i, 0)), pl.BlockSpec((1, part), lambda i: (0, i))],
        out_shape=[
            jax.ShapeDtypeStruct((rows, width), jnp.bfloat16),
            jax.ShapeDtypeStruct((1, width), jnp.float32),
        ],
        compiler_params=params(),
        cost_estimate=pl.CostEstimate(flops=2**27, bytes_accessed=6 * 2**20, transcendentals=rows),
    )(tokens, w_out, score_w)


def project_kernel(place_ref, normed_ref, w_ref, *rest):
    x = 0.5 * jnp.dot(normed_ref[...], w_ref[0], preferred_element_type=jnp.float32)
    rest[-1][...] = (x + x * jnp.tanh(x)).astype(jnp.bfloat16)


def project(normed, blocks, place, total, into=None):
    rows, width = normed.shape
    many, _, columns = blocks.shape
    more = into is not None
    return pl.pallas_call(
        project_kernel,
        grid_spec=pltpu.PrefetchScalarGridSpec(
            num_scalar_prefetch=1,
            grid=(many,),
            in_specs=[
                pl.BlockSpec((rows, width), lambda j, o: (0, 0)),
                pl.BlockSpec((1, width, columns), lambda j, o: (j, 0, 0)),
            ]
            + [pl.BlockSpec(memory_space=pl.ANY)] * more,
            out_specs=pl.BlockSpec((rows, columns), lambda j, o: (0, o[j])),
        ),
        out_shape=jax.ShapeDtypeStruct((rows, total), jnp.bfloat16),
        input_output_aliases={3: 0} if more else {},
        compiler_params=params(),
        cost_estimate=pl.CostEstimate(
            flops=2 * rows * width * many * columns, bytes_accessed=5 * 2**20, transcendentals=rows * many * columns
        ),
    )(place, normed, blocks, *([into] if more else []))


def copies_kernel(*refs):
    ins, out, held, into, back = refs[:-4], refs[-4], refs[-3], refs[-2], refs[-1]
    reads = [pltpu.make_async_copy(ref, held.at[j], into.at[j]) for j, ref in enumerate(ins)]
    for read in reads:
        read.start()
    writes = []
    for j, read in enumerate(reads):
        read.wait()
        for i in range(out.shape[0]):
            write = pltpu.make_async_copy(held.at[j], out.at[i, j], back.at[i, j])
            write.start()
            writes.append(write)
    for write in writes:
        write.wait()


def copies(times, *blocks):
    held = (len(blocks),) + blocks[0].shape
    return pl.pallas_call(
        copies_kernel,
        in_specs=[pl.BlockSpec(memory_space=pl.ANY)] * len(blocks),
        out_specs=pl.BlockSpec(memory_space=pl.ANY),
        out_shape=jax.ShapeDtypeStruct((times,) + held, blocks[0].dtype),
        scratch_shapes=[
            pltpu.VMEM(held, blocks[0].dtype),
            pltpu.SemaphoreType.DMA((len(blocks),)),
            pltpu.SemaphoreType.DMA((times, len(blocks))),
        ],
        compiler_params=params(),
        cost_estimate=pl.CostEstimate(flops=0, bytes_accessed=2**22, transcendentals=0),
    )(*blocks)


def side_by_side(refs):
    blocks = [ref[...].reshape(-1, ref.shape[-1]) for ref in refs]
    return jnp.concatenate(blocks, axis=0) if len(blocks) > 1 else blocks[0]


def weigh(q, k, v, factor):
    s = lax.dot_general(q, k, (((1,), (1,)), ((), ())), preferred_element_type=jnp.float32)
    w = (s * jnp.tanh(s * (0.5 * factor)) + s).astype(jnp.bfloat16)
    return jnp.dot(w, v, preferred_element_type=jnp.float32)


def partial_kernel(*refs, count, factor, tile, more):
    q_ref, ks, vs, out_ref = refs[0], refs[1 : 1 + count], refs[1 + count : 1 + 2 * count], refs[-1]
    k, v = side_by_side(ks), side_by_side(vs)
    for r in range(0, q_ref.shape[0], tile):
        sums = weigh(q_ref[r : r + tile, :], k, v, factor)
        if more:
            sums += refs[-2][r : r + tile, :]
        out_ref[r : r + tile, :] = sums


def key_specs(arrays, head, column):
    keys = [pl.BlockSpec((a.shape[0], a.shape[1] // 2, head), lambda h: (0, 0, column(h))) for a in arrays]
    values = [pl.BlockSpec((a.shape[0], a.shape[1] // 2, head), lambda h: (0, 1, column(h))) for a in arrays]
    return keys + values


def attend_part(proj, first, arrays, before=None):
    rows, head = proj.shape[0], proj.shape[1] // (2 * HEADS)
    heads = arrays[0].shape[2] // head
    keys = sum(a.shape[0] * a.shape[1] // 2 for a in arrays)
    sums = pl.BlockSpec((rows, head), lambda h: (0, h))
    more = before is not None
    return pl.pallas_call(
        functools.partial(partial_kernel, count=len(arrays), factor=float(head) ** -0.5, tile=256, more=more),
        grid=(heads,),
        in_specs=[pl.BlockSpec((rows, head), lambda h: (0, HEADS + first + h))]
        + key_specs(arrays, head, lambda h: h)
        + [sums] * more,
        out_specs=sums,
        out_shape=jax.ShapeDtypeStruct((rows, heads * head), jnp.float32),
        compiler_params=params(),
        cost_estimate=pl.CostEstimate(
            flops=8 * rows * keys * heads * head, bytes_accessed=4 * 2**20, transcendentals=rows * keys * heads
        ),
    )(proj, *arrays, *arrays, *([before] if more else []))


def finish_kernel(*refs, count, factor, tile):
    q_ref, ks, vs = refs[0], refs[1 : 1 + count], refs[1 + count : 1 + 2 * count]
    sums_ref, done_ref, gate_ref, tokens_ref, ws_ref, sw_ref, scale_ref, live_ref, gated_ref, score_ref, attn = refs[1 + 2 * count :]
    h = pl.program_id(0)
    rows = q_ref.shape[0]
    k, v = side_by_side(ks), side_by_side(vs)
    for r in range(0, rows, tile):
        attn[h, r : r + tile, :] = weigh(q_ref[r : r + tile, :], k, v, factor) + sums_ref[r : r + tile, :]

    @pl.when(h == pl.num_programs(0) - 1)
    def _():
        for r in range(0, rows, tile):
            heads = [attn[i, r : r + tile, :] for i in range(attn.shape[0])] + [done_ref[r : r + tile, :]]
            whole = jnp.concatenate(heads, axis=1) * scale_ref[0]
            gated = (layer_norm(whole) * gate_ref[r : r + tile, :].astype(jnp.float32)).astype(jnp.bfloat16)
            gated_ref[r : r + tile, :] = gated
            total = gated.astype(jnp.float32) * ws_ref[...]
            total += tokens_ref[r : r + tile, :].astype(jnp.float32) * sw_ref[...]
            slots = r + lax.broadcasted_iota(jnp.int32, (1, tile), 1)
            score = jnp.sum(total, axis=-1).reshape(1, -1)
            score = jnp.where(slots < live_ref[0], score, 0.0)
            score_ref[:, :, r : r + tile] = jnp.broadcast_to(score[None], (score_ref.shape[0], 1, tile))


def finish(proj, arrays, sums, done, tokens, ws, score_w, scale, live, parts):
    rows, width = tokens.shape
    head = width // HEADS
    left = arrays[0].shape[2] // head
    whole = pl.BlockSpec((rows, width), lambda h: (0, 0))
    line = pl.BlockSpec((1, width), lambda h: (0, 0))
    return pl.pallas_call(
        functools.partial(finish_kernel, count=len(arrays), factor=float(head) ** -0.5, tile=256),
        grid=(left,),
        in_specs=[pl.BlockSpec((rows, head), lambda h: (0, HEADS + h))]
        + key_specs(arrays, head, lambda h: h)
        + [
            pl.BlockSpec((rows, head), lambda h: (0, h)),
            pl.BlockSpec(done.shape, lambda h: (0, 0)),
            whole,
            whole,
            line,
            line,
            pl.BlockSpec(memory_space=pltpu.SMEM),
            pl.BlockSpec(memory_space=pltpu.SMEM),
        ],
        out_specs=[whole, pl.BlockSpec((parts, 1, rows), lambda h: (0, 0, 0))],
        out_shape=[
            jax.ShapeDtypeStruct((rows, width), jnp.bfloat16),
            jax.ShapeDtypeStruct((parts, 1, rows), jnp.float32),
        ],
        scratch_shapes=[pltpu.VMEM((left, rows, head), jnp.float32)],
        compiler_params=params(),
        cost_estimate=pl.CostEstimate(flops=2**32, bytes_accessed=12 * 2**20, transcendentals=2**22),
    )(proj, *arrays, *arrays, sums, done, proj, tokens, ws, score_w, scale, live)


def out_kernel(gated_ref, w_ref, tokens_ref, out_ref):
    y = tokens_ref[...].astype(jnp.float32) + jnp.dot(gated_ref[...], w_ref[...], preferred_element_type=jnp.float32)
    out_ref[...] = y.astype(jnp.bfloat16)


def project_out(gated, w_out, tokens, tile=256):
    rows, width = tokens.shape
    return pl.pallas_call(
        out_kernel,
        grid=(rows // tile,),
        in_specs=[
            pl.BlockSpec((tile, width), lambda i: (i, 0)),
            pl.BlockSpec((width, width), lambda i: (0, 0)),
            pl.BlockSpec((tile, width), lambda i: (i, 0)),
        ],
        out_specs=pl.BlockSpec((tile, width), lambda i: (i, 0)),
        out_shape=jax.ShapeDtypeStruct((rows, width), jnp.bfloat16),
        compiler_params=params(),
        cost_estimate=pl.CostEstimate(flops=2 * rows * width * width, bytes_accessed=7 * 2**20, transcendentals=0),
    )(gated, w_out, tokens)


def pick_kernel(index_ref, table_ref, out_ref):
    index = index_ref[...]
    count = index.shape[0]
    height, lanes = table_ref.shape
    onehot = (lax.broadcasted_iota(jnp.int32, (count, height), 1) == index // lanes).astype(jnp.bfloat16)
    rest = table_ref[...]
    rows = jnp.zeros((count, lanes), jnp.float32)
    for _ in range(3):
        part = rest.astype(jnp.bfloat16)
        rows += jnp.dot(onehot, part, preferred_element_type=jnp.float32)
        rest = rest - part.astype(jnp.float32)
    mine = lax.broadcasted_iota(jnp.int32, (count, lanes), 1) == index % lanes
    out_ref[...] = jnp.sum(jnp.where(mine, rows, 0.0), axis=-1).reshape(1, -1)


def pick(index, table):
    count = index.shape[0]
    return pl.pallas_call(
        pick_kernel,
        out_shape=jax.ShapeDtypeStruct((1, count), jnp.float32),
        compiler_params=params(),
    )(index.reshape(count, 1), table.reshape(-1, 128))


HEADS_A = 5
tie = lax.optimization_barrier


def shift(block, axis, step):
    return lax.ppermute(block, axis, shifted(lax.axis_size(axis), step))


def on_device(
    cand_tokens, hist_keys, hist_values, hist_len, cand_count, impressions, w_proj, w_out, score_w
):
    tokens = cand_tokens[0]
    rows, width = tokens.shape
    own = hist_keys.shape[1]
    head = width // HEADS
    cand = lax.axis_index(("z", "x"))
    core = lax.axis_index("core")
    many_y, many_core = lax.axis_size("y"), lax.axis_size("core")
    parts, many_z, many_x = lax.axis_size(("z", "x")), lax.axis_size("z"), lax.axis_size("x")

    position = cand * own + jnp.arange(own, dtype=jnp.int32)
    keys = jnp.where((position < hist_len[0])[:, None], hist_keys[0], jnp.zeros((), jnp.bfloat16))
    values = hist_values[0]
    cut = HEADS_A * head
    mine_a = jnp.concatenate([keys[:, :cut], values[:, :cut]], axis=0)
    mine_b = jnp.concatenate([keys[:, cut:], values[:, cut:]], axis=0)

    xs = [mine_a, shift(mine_a, "x", 1), shift(mine_a, "x", -1), shift(mine_a, "x", 2)]
    zs = lax.all_to_all(copies(many_z, mine_b)[:, 0], "z", split_axis=0, concat_axis=0, tiled=True)
    w_near = [w_proj, shift(w_proj, "y", 1), shift(w_proj, "y", -1)]
    w_far, xs, w_near = tie((w_proj, xs, w_near))
    w_parts = w_near + [shift(w_far, "y", 2)]
    normed, ws = prepare(tokens, w_out, score_w[None, :])

    p = q = start = copies(1, *xs)[0]
    zs = copies(many_x, zs)[:, 0]
    p, q, w_parts, normed, zs = tie((shift(p, "z", 1), shift(q, "z", -1), w_parts, normed, zs))
    w_mine = copies(1, *w_parts)[0]
    b = lax.all_to_all(zs, "x", split_axis=0, concat_axis=0, tiled=True)
    b = b.reshape(-1, *mine_b.shape)
    block = (lax.axis_index("y") - jnp.array([0, 1, -1, 2])) % many_y * many_core
    proj = project(normed, w_mine, (block + core).astype(jnp.int32), 2 * width)
    w_other = lax.ppermute(w_mine, "core", [(0, 1), (1, 0)])
    near = [start, p, q]
    p, q = shift(p, "z", 1), shift(q, "z", -1)
    proj = project(normed, w_other, (block + 1 - core).astype(jnp.int32), 2 * width, proj)
    p, q, proj = tie((p, q, proj))
    middle = [p, q]
    p, q = shift(p, "z", 1), shift(q, "z", -1)
    sums = attend_part(proj, 0, near)
    p, q, sums = tie((p, q, sums))
    half = many_x // 2
    far = [p, q, shift(p[:half], "z", 1), shift(q[half:], "z", -1)]
    sums = attend_part(proj, 0, middle, sums)
    done = attend_part(proj, HEADS_A, [b])

    scale = 0.5 * float(head) ** -0.5 / hist_len.astype(jnp.float32)
    live = cand_count - cand * rows
    gated, sent = finish(proj, far, sums, done, tokens, ws, score_w[None, :], scale, live, parts)
    every = lax.all_to_all(sent, ("z", "x"), split_axis=0, concat_axis=0, tiled=True)
    layer_out = project_out(gated, w_out, tokens)
    ranked = pick(impressions[0], every)
    return (layer_out[None], ranked)


def solution(mesh):
    split = Mesh(mesh.devices.reshape(4, 2, 8, 4), ("y", "core", "z", "x"))
    users, cands = ("y", "core"), ("z", "x")
    return jax.shard_map(
        on_device,
        mesh=split,
        in_specs=(
            P(users, cands, None),
            P(users, cands, None),
            P(users, cands, None),
            P(users),
            P(users),
            P(users, cands),
            P(None, users),
            P(),
            P(),
        ),
        out_specs=(P(users, cands, None), P(users, cands)),
        check_vma=False,
    )
```

```python
import functools

import jax
import jax.numpy as jnp
from jax import lax
from jax.experimental import pallas as pl
from jax.experimental.pallas import tpu as pltpu
from jax.sharding import Mesh
from jax.sharding import PartitionSpec as P

HEADS = 8
eps = 1e-05
VMEM_LIMIT = 24 * 2**20


def params():
    return pltpu.CompilerParams(vmem_limit_bytes=VMEM_LIMIT)


def layer_norm(values):
    mean = jnp.mean(values, axis=-1, keepdims=True)
    centered = values - mean
    var = jnp.mean(centered * centered, axis=-1, keepdims=True)
    return centered * lax.rsqrt(var + eps)


def shifted(size, step):
    return [(i, (i + step) % size) for i in range(size)]


def prepare_kernel(tokens_ref, w_ref, sw_ref, normed_ref, ws_ref):
    normed_ref[...] = layer_norm(tokens_ref[...].astype(jnp.float32)).astype(jnp.bfloat16)
    ws_ref[...] = lax.dot_general(
        sw_ref[...],
        w_ref[...].astype(jnp.float32),
        (((1,), (1,)), ((), ())),
        precision=lax.Precision.HIGHEST,
        preferred_element_type=jnp.float32,
    )


def prepare(tokens, w_out, score_w, steps=4):
    rows, width = tokens.shape
    tile, part = rows // steps, width // steps
    return pl.pallas_call(
        prepare_kernel,
        grid=(steps,),
        in_specs=[
            pl.BlockSpec((tile, width), lambda i: (i, 0)),
            pl.BlockSpec((part, width), lambda i: (i, 0)),
            pl.BlockSpec((1, width), lambda i: (0, 0)),
        ],
        out_specs=[pl.BlockSpec((tile, width), lambda i: (i, 0)), pl.BlockSpec((1, part), lambda i: (0, i))],
        out_shape=[
            jax.ShapeDtypeStruct((rows, width), jnp.bfloat16),
            jax.ShapeDtypeStruct((1, width), jnp.float32),
        ],
        compiler_params=params(),
        cost_estimate=pl.CostEstimate(flops=2**27, bytes_accessed=6 * 2**20, transcendentals=rows),
    )(tokens, w_out, score_w)


def project_kernel(place_ref, normed_ref, first_ref, second_ref, *rest, count):
    w = jnp.where(pl.program_id(0) < count, first_ref[0], second_ref[0])
    x = 0.5 * jnp.dot(normed_ref[...], w, preferred_element_type=jnp.float32)
    rest[-1][...] = (x + x * jnp.tanh(x)).astype(jnp.bfloat16)


def project(normed, first, second, place, total, into=None):
    rows, width = normed.shape
    count, _, columns = first.shape
    many = count + second.shape[0]
    more = into is not None
    return pl.pallas_call(
        functools.partial(project_kernel, count=count),
        grid_spec=pltpu.PrefetchScalarGridSpec(
            num_scalar_prefetch=1,
            grid=(many,),
            in_specs=[
                pl.BlockSpec((rows, width), lambda j, o: (0, 0)),
                pl.BlockSpec((1, width, columns), lambda j, o: (jnp.minimum(j, count - 1), 0, 0)),
                pl.BlockSpec((1, width, columns), lambda j, o: (jnp.maximum(j - count, 0), 0, 0)),
            ]
            + [pl.BlockSpec(memory_space=pl.ANY)] * more,
            out_specs=pl.BlockSpec((rows, columns), lambda j, o: (0, o[j])),
        ),
        out_shape=jax.ShapeDtypeStruct((rows, total), jnp.bfloat16),
        input_output_aliases={4: 0} if more else {},
        compiler_params=params(),
        cost_estimate=pl.CostEstimate(
            flops=2 * rows * width * many * columns, bytes_accessed=5 * 2**20, transcendentals=rows * many * columns
        ),
    )(place, normed, first, second, *([into] if more else []))


def copies_kernel(*refs):
    ins, out, held, into, back = refs[:-4], refs[-4], refs[-3], refs[-2], refs[-1]
    reads = [pltpu.make_async_copy(ref, held.at[j], into.at[j]) for j, ref in enumerate(ins)]
    for read in reads:
        read.start()
    writes = []
    for j, read in enumerate(reads):
        read.wait()
        for i in range(out.shape[0]):
            write = pltpu.make_async_copy(held.at[j], out.at[i, j], back.at[i, j])
            write.start()
            writes.append(write)
    for write in writes:
        write.wait()


def copies(times, *blocks):
    held = (len(blocks),) + blocks[0].shape
    return pl.pallas_call(
        copies_kernel,
        in_specs=[pl.BlockSpec(memory_space=pl.ANY)] * len(blocks),
        out_specs=pl.BlockSpec(memory_space=pl.ANY),
        out_shape=jax.ShapeDtypeStruct((times,) + held, blocks[0].dtype),
        scratch_shapes=[
            pltpu.VMEM(held, blocks[0].dtype),
            pltpu.SemaphoreType.DMA((len(blocks),)),
            pltpu.SemaphoreType.DMA((times, len(blocks))),
        ],
        compiler_params=params(),
        cost_estimate=pl.CostEstimate(flops=0, bytes_accessed=2**22, transcendentals=0),
    )(*blocks)


def side_by_side(refs):
    blocks = [ref[...].reshape(-1, ref.shape[-1]) for ref in refs]
    return jnp.concatenate(blocks, axis=0) if len(blocks) > 1 else blocks[0]


def weigh(q, k, v, factor):
    s = lax.dot_general(q, k, (((1,), (1,)), ((), ())), preferred_element_type=jnp.float32)
    w = (s * jnp.tanh(s * (0.5 * factor)) + s).astype(jnp.bfloat16)
    return jnp.dot(w, v, preferred_element_type=jnp.float32)


def partial_kernel(*refs, count, factor, tile, more):
    q_ref, ks, vs, out_ref = refs[0], refs[1 : 1 + count], refs[1 + count : 1 + 2 * count], refs[-1]
    k, v = side_by_side(ks), side_by_side(vs)
    for r in range(0, q_ref.shape[0], tile):
        sums = weigh(q_ref[r : r + tile, :], k, v, factor)
        if more:
            sums += refs[-2][r : r + tile, :]
        out_ref[r : r + tile, :] = sums


def key_specs(arrays, head, column):
    keys = [pl.BlockSpec((a.shape[0], a.shape[1] // 2, head), lambda h: (0, 0, column(h))) for a in arrays]
    values = [pl.BlockSpec((a.shape[0], a.shape[1] // 2, head), lambda h: (0, 1, column(h))) for a in arrays]
    return keys + values


def attend_part(proj, first, arrays, before=None):
    rows, head = proj.shape[0], proj.shape[1] // (2 * HEADS)
    heads = arrays[0].shape[2] // head
    keys = sum(a.shape[0] * a.shape[1] // 2 for a in arrays)
    sums = pl.BlockSpec((rows, head), lambda h: (0, h))
    more = before is not None
    return pl.pallas_call(
        functools.partial(partial_kernel, count=len(arrays), factor=float(head) ** -0.5, tile=256, more=more),
        grid=(heads,),
        in_specs=[pl.BlockSpec((rows, head), lambda h: (0, HEADS + first + h))]
        + key_specs(arrays, head, lambda h: h)
        + [sums] * more,
        out_specs=sums,
        out_shape=jax.ShapeDtypeStruct((rows, heads * head), jnp.float32),
        compiler_params=params(),
        cost_estimate=pl.CostEstimate(
            flops=8 * rows * keys * heads * head, bytes_accessed=4 * 2**20, transcendentals=rows * keys * heads
        ),
    )(proj, *arrays, *arrays, *([before] if more else []))


def finish_kernel(*refs, count, factor, tile):
    q_ref, ks, vs = refs[0], refs[1 : 1 + count], refs[1 + count : 1 + 2 * count]
    sums_ref, done_ref, gate_ref, tokens_ref, ws_ref, sw_ref, scale_ref, live_ref, gated_ref, score_ref, attn = refs[1 + 2 * count :]
    h = pl.program_id(0)
    rows = q_ref.shape[0]
    k, v = side_by_side(ks), side_by_side(vs)
    for r in range(0, rows, tile):
        attn[h, r : r + tile, :] = weigh(q_ref[r : r + tile, :], k, v, factor) + sums_ref[r : r + tile, :]

    @pl.when(h == pl.num_programs(0) - 1)
    def _():
        for r in range(0, rows, tile):
            heads = [attn[i, r : r + tile, :] for i in range(attn.shape[0])] + [done_ref[r : r + tile, :]]
            whole = jnp.concatenate(heads, axis=1) * scale_ref[0]
            gated = (layer_norm(whole) * gate_ref[r : r + tile, :].astype(jnp.float32)).astype(jnp.bfloat16)
            gated_ref[r : r + tile, :] = gated
            total = gated.astype(jnp.float32) * ws_ref[...]
            total += tokens_ref[r : r + tile, :].astype(jnp.float32) * sw_ref[...]
            slots = r + lax.broadcasted_iota(jnp.int32, (1, tile), 1)
            score = jnp.sum(total, axis=-1).reshape(1, -1)
            score = jnp.where(slots < live_ref[0], score, 0.0)
            score_ref[:, :, r : r + tile] = jnp.broadcast_to(score[None], (score_ref.shape[0], 1, tile))


def finish(proj, arrays, sums, done, tokens, ws, score_w, scale, live, parts):
    rows, width = tokens.shape
    head = width // HEADS
    left = arrays[0].shape[2] // head
    whole = pl.BlockSpec((rows, width), lambda h: (0, 0))
    line = pl.BlockSpec((1, width), lambda h: (0, 0))
    return pl.pallas_call(
        functools.partial(finish_kernel, count=len(arrays), factor=float(head) ** -0.5, tile=256),
        grid=(left,),
        in_specs=[pl.BlockSpec((rows, head), lambda h: (0, HEADS + h))]
        + key_specs(arrays, head, lambda h: h)
        + [
            pl.BlockSpec((rows, head), lambda h: (0, h)),
            pl.BlockSpec(done.shape, lambda h: (0, 0)),
            whole,
            whole,
            line,
            line,
            pl.BlockSpec(memory_space=pltpu.SMEM),
            pl.BlockSpec(memory_space=pltpu.SMEM),
        ],
        out_specs=[whole, pl.BlockSpec((parts, 1, rows), lambda h: (0, 0, 0))],
        out_shape=[
            jax.ShapeDtypeStruct((rows, width), jnp.bfloat16),
            jax.ShapeDtypeStruct((parts, 1, rows), jnp.float32),
        ],
        scratch_shapes=[pltpu.VMEM((left, rows, head), jnp.float32)],
        compiler_params=params(),
        cost_estimate=pl.CostEstimate(flops=2**32, bytes_accessed=12 * 2**20, transcendentals=2**22),
    )(proj, *arrays, *arrays, sums, done, proj, tokens, ws, score_w, scale, live)


def out_kernel(gated_ref, w_ref, tokens_ref, out_ref):
    y = tokens_ref[...].astype(jnp.float32) + jnp.dot(gated_ref[...], w_ref[...], preferred_element_type=jnp.float32)
    out_ref[...] = y.astype(jnp.bfloat16)


def project_out(gated, w_out, tokens, tile=256):
    rows, width = tokens.shape
    return pl.pallas_call(
        out_kernel,
        grid=(rows // tile,),
        in_specs=[
            pl.BlockSpec((tile, width), lambda i: (i, 0)),
            pl.BlockSpec((width, width), lambda i: (0, 0)),
            pl.BlockSpec((tile, width), lambda i: (i, 0)),
        ],
        out_specs=pl.BlockSpec((tile, width), lambda i: (i, 0)),
        out_shape=jax.ShapeDtypeStruct((rows, width), jnp.bfloat16),
        compiler_params=params(),
        cost_estimate=pl.CostEstimate(flops=2 * rows * width * width, bytes_accessed=7 * 2**20, transcendentals=0),
    )(gated, w_out, tokens)


def pick_kernel(index_ref, table_ref, out_ref):
    index = index_ref[...]
    count = index.shape[0]
    height, lanes = table_ref.shape
    onehot = (lax.broadcasted_iota(jnp.int32, (count, height), 1) == index // lanes).astype(jnp.bfloat16)
    rest = table_ref[...]
    rows = jnp.zeros((count, lanes), jnp.float32)
    for _ in range(3):
        part = rest.astype(jnp.bfloat16)
        rows += jnp.dot(onehot, part, preferred_element_type=jnp.float32)
        rest = rest - part.astype(jnp.float32)
    mine = lax.broadcasted_iota(jnp.int32, (count, lanes), 1) == index % lanes
    out_ref[...] = jnp.sum(jnp.where(mine, rows, 0.0), axis=-1).reshape(1, -1)


def pick(index, table):
    count = index.shape[0]
    return pl.pallas_call(
        pick_kernel,
        out_shape=jax.ShapeDtypeStruct((1, count), jnp.float32),
        compiler_params=params(),
    )(index.reshape(count, 1), table.reshape(-1, 128))


HEADS_A = 5
tie = lax.optimization_barrier


def shift(block, axis, step):
    return lax.ppermute(block, axis, shifted(lax.axis_size(axis), step))


def on_device(
    cand_tokens, hist_keys, hist_values, hist_len, cand_count, impressions, w_proj, w_out, score_w
):
    tokens = cand_tokens[0]
    rows, width = tokens.shape
    own = hist_keys.shape[1]
    head = width // HEADS
    cand = lax.axis_index(("z", "x"))
    core = lax.axis_index("core")
    many_y, many_core = lax.axis_size("y"), lax.axis_size("core")
    parts, many_z, many_x = lax.axis_size(("z", "x")), lax.axis_size("z"), lax.axis_size("x")

    position = cand * own + jnp.arange(own, dtype=jnp.int32)
    keys = jnp.where((position < hist_len[0])[:, None], hist_keys[0], jnp.zeros((), jnp.bfloat16))
    values = hist_values[0]
    cut = HEADS_A * head
    mine_a = jnp.concatenate([keys[:, :cut], values[:, :cut]], axis=0)
    mine_b = jnp.concatenate([keys[:, cut:], values[:, cut:]], axis=0)

    xs = [mine_a, shift(mine_a, "x", 1), shift(mine_a, "x", -1), shift(mine_a, "x", 2)]
    zs = lax.all_to_all(copies(many_z, mine_b)[:, 0], "z", split_axis=0, concat_axis=0, tiled=True)
    w_near = [w_proj, shift(w_proj, "y", 1), shift(w_proj, "y", -1)]
    w_far, xs, w_near = tie((w_proj, xs, w_near))
    w_far = shift(w_far, "y", 2)
    swap = [(0, 1), (1, 0)]
    w_near = copies(1, *w_near)[0]
    w_other = lax.ppermute(w_near, "core", swap)
    normed, ws = prepare(tokens, w_out, score_w[None, :])

    p = q = start = copies(1, *xs)[0]
    zs = copies(many_x, zs)[:, 0]
    p, q, w_far, normed, w_other, _ = tie((shift(p, "z", 1), shift(q, "z", -1), w_far, normed, w_other, zs))
    b = lax.all_to_all(zs, "x", split_axis=0, concat_axis=0, tiled=True)
    b = b.reshape(-1, *mine_b.shape)
    w_far_other = lax.ppermute(w_far, "core", swap)
    near = [start, p, q]
    p, q = shift(p, "z", 1), shift(q, "z", -1)
    block = (lax.axis_index("y") - jnp.array([0, 1, -1, 2])) % many_y * many_core
    mine, other = (block + core).astype(jnp.int32), (block + 1 - core).astype(jnp.int32)
    proj = project(normed, w_near, w_other, jnp.concatenate([mine[:3], other[:3]]), 2 * width)
    proj = project(normed, w_far[None], w_far_other[None], jnp.concatenate([mine[3:], other[3:]]), 2 * width, proj)
    p, q, proj = tie((p, q, proj))
    near += [p, q]
    p, q = shift(p, "z", 1), shift(q, "z", -1)
    sums = attend_part(proj, 0, near)
    p, q, sums = tie((p, q, sums))
    ring = [(c * many_z + i, c * many_z + (i + (1, -1)[c]) % many_z) for c in range(2) for i in range(many_z)]
    far = [p, q, lax.ppermute(jnp.where(core == 0, p, q), ("core", "z"), ring)]
    done = attend_part(proj, HEADS_A, [b])

    scale = 0.5 * float(head) ** -0.5 / hist_len.astype(jnp.float32)
    live = cand_count - cand * rows
    gated, sent = finish(proj, far, sums, done, tokens, ws, score_w[None, :], scale, live, parts)
    every = lax.all_to_all(sent, ("z", "x"), split_axis=0, concat_axis=0, tiled=True)
    layer_out = project_out(gated, w_out, tokens)
    ranked = pick(impressions[0], every)
    return (layer_out[None], ranked)


def solution(mesh):
    split = Mesh(mesh.devices.reshape(4, 2, 8, 4), ("y", "core", "z", "x"))
    users, cands = ("y", "core"), ("z", "x")
    return jax.shard_map(
        on_device,
        mesh=split,
        in_specs=(
            P(users, cands, None),
            P(users, cands, None),
            P(users, cands, None),
            P(users),
            P(users),
            P(users, cands),
            P(None, users),
            P(),
            P(),
        ),
        out_specs=(P(users, cands, None), P(users, cands)),
        check_vma=False,
    )
```

```python
import functools

import jax
import jax.numpy as jnp
from jax import lax
from jax.experimental import pallas as pl
from jax.experimental.pallas import tpu as pltpu
from jax.sharding import Mesh
from jax.sharding import PartitionSpec as P

HEADS = 8
eps = 1e-05
VMEM_LIMIT = 24 * 2**20
VMEM_MOST = 58 * 2**20


def params(limit=VMEM_LIMIT):
    return pltpu.CompilerParams(vmem_limit_bytes=limit)


def layer_norm(values):
    mean = jnp.mean(values, axis=-1, keepdims=True)
    centered = values - mean
    var = jnp.mean(centered * centered, axis=-1, keepdims=True)
    return centered * lax.rsqrt(var + eps)


def shifted(size, step):
    return [(i, (i + step) % size) for i in range(size)]


def prepare_kernel(tokens_ref, w_ref, sw_ref, normed_ref, ws_ref, base_ref):
    tokens = tokens_ref[...].astype(jnp.float32)
    normed_ref[...] = layer_norm(tokens).astype(jnp.bfloat16)
    base_ref[...] = jnp.sum(tokens * sw_ref[...], axis=-1).reshape(1, 1, -1)

    @pl.when(pl.program_id(0) == 0)
    def _():
        ws_ref[...] = lax.dot_general(
            sw_ref[...],
            w_ref[...].astype(jnp.float32),
            (((1,), (1,)), ((), ())),
            precision=lax.Precision.HIGHEST,
            preferred_element_type=jnp.float32,
        )


def prepare(tokens, w_out, score_w, steps=3):
    rows, width = tokens.shape
    tile, part = rows // steps, width
    return pl.pallas_call(
        prepare_kernel,
        grid=(steps,),
        in_specs=[
            pl.BlockSpec((tile, width), lambda i: (i, 0)),
            pl.BlockSpec((part, width), lambda i: (0, 0)),
            pl.BlockSpec((1, width), lambda i: (0, 0)),
        ],
        out_specs=[
            pl.BlockSpec((tile, width), lambda i: (i, 0)),
            pl.BlockSpec((1, part), lambda i: (0, 0)),
            pl.BlockSpec((1, 1, tile), lambda i: (i, 0, 0)),
        ],
        out_shape=[
            jax.ShapeDtypeStruct((rows, width), jnp.bfloat16),
            jax.ShapeDtypeStruct((1, width), jnp.float32),
            jax.ShapeDtypeStruct((steps, 1, tile), jnp.float32),
        ],
        compiler_params=params(),
        cost_estimate=pl.CostEstimate(flops=2**27, bytes_accessed=6 * 2**20, transcendentals=rows),
    )(tokens, w_out, score_w)


def project_kernel(place_ref, normed_ref, first_ref, second_ref, *rest, count):
    w = jnp.where(pl.program_id(0) < count, first_ref[0], second_ref[0])
    x = 0.5 * jnp.dot(normed_ref[...], w, preferred_element_type=jnp.float32)
    rest[-1][...] = (x + x * jnp.tanh(x)).astype(jnp.bfloat16)


def project(normed, first, second, place, total, into=None):
    rows, width = normed.shape
    count, _, columns = first.shape
    many = count + second.shape[0]
    more = into is not None
    return pl.pallas_call(
        functools.partial(project_kernel, count=count),
        grid_spec=pltpu.PrefetchScalarGridSpec(
            num_scalar_prefetch=1,
            grid=(many,),
            in_specs=[
                pl.BlockSpec((rows, width), lambda j, o: (0, 0)),
                pl.BlockSpec((1, width, columns), lambda j, o: (jnp.minimum(j, count - 1), 0, 0)),
                pl.BlockSpec((1, width, columns), lambda j, o: (jnp.maximum(j - count, 0), 0, 0)),
            ]
            + [pl.BlockSpec(memory_space=pl.ANY)] * more,
            out_specs=pl.BlockSpec((rows, columns), lambda j, o: (0, o[j])),
        ),
        out_shape=jax.ShapeDtypeStruct((rows, total), jnp.bfloat16),
        input_output_aliases={4: 0} if more else {},
        compiler_params=params(),
        cost_estimate=pl.CostEstimate(
            flops=2 * rows * width * many * columns, bytes_accessed=5 * 2**20, transcendentals=rows * many * columns
        ),
    )(place, normed, first, second, *([into] if more else []))


def copies_kernel(*refs):
    ins, out, held, into, back = refs[:-4], refs[-4], refs[-3], refs[-2], refs[-1]
    reads = [pltpu.make_async_copy(ref, held.at[j], into.at[j]) for j, ref in enumerate(ins)]
    for read in reads:
        read.start()
    writes = []
    for j, read in enumerate(reads):
        read.wait()
        for i in range(out.shape[0]):
            write = pltpu.make_async_copy(held.at[j], out.at[i, j], back.at[i, j])
            write.start()
            writes.append(write)
    for write in writes:
        write.wait()


def copies(times, *blocks):
    held = (len(blocks),) + blocks[0].shape
    return pl.pallas_call(
        copies_kernel,
        in_specs=[pl.BlockSpec(memory_space=pl.ANY)] * len(blocks),
        out_specs=pl.BlockSpec(memory_space=pl.ANY),
        out_shape=jax.ShapeDtypeStruct((times,) + held, blocks[0].dtype),
        scratch_shapes=[
            pltpu.VMEM(held, blocks[0].dtype),
            pltpu.SemaphoreType.DMA((len(blocks),)),
            pltpu.SemaphoreType.DMA((times, len(blocks))),
        ],
        compiler_params=params(),
        cost_estimate=pl.CostEstimate(flops=0, bytes_accessed=2**22, transcendentals=0),
    )(*blocks)


def stage_kernel(live_ref, keys_ref, values_ref, a_ref, b_ref, *, cut):
    own = keys_ref.shape[0]
    valid = lax.broadcasted_iota(jnp.int32, keys_ref.shape, 0) < live_ref[0]
    keys = jnp.where(valid, keys_ref[...], jnp.zeros((), keys_ref.dtype))
    values = values_ref[...]
    a_ref[:own], a_ref[own:] = keys[:, :cut], values[:, :cut]
    for i in range(b_ref.shape[0]):
        b_ref[i, :own], b_ref[i, own:] = keys[:, cut:], values[:, cut:]


def stage(live, keys, values, cut, times):
    own, width = keys.shape
    return pl.pallas_call(
        functools.partial(stage_kernel, cut=cut),
        in_specs=[
            pl.BlockSpec(memory_space=pltpu.SMEM),
            pl.BlockSpec(memory_space=pltpu.VMEM),
            pl.BlockSpec(memory_space=pltpu.VMEM),
        ],
        out_shape=[
            jax.ShapeDtypeStruct((2 * own, cut), keys.dtype),
            jax.ShapeDtypeStruct((times, 2 * own, width - cut), keys.dtype),
        ],
        compiler_params=params(VMEM_MOST),
    )(live, keys, values)


def side_by_side(refs):
    blocks = [ref[...].reshape(-1, ref.shape[-1]) for ref in refs]
    return jnp.concatenate(blocks, axis=0) if len(blocks) > 1 else blocks[0]


def weigh(q, k, v, factor):
    s = lax.dot_general(q, k, (((1,), (1,)), ((), ())), preferred_element_type=jnp.float32)
    w = (s * jnp.tanh(s * (0.5 * factor)) + s).astype(jnp.bfloat16)
    return jnp.dot(w, v, preferred_element_type=jnp.float32)


def partial_kernel(*refs, count, factor, tile, more):
    q_ref, ks, vs, out_ref = refs[0], refs[1 : 1 + count], refs[1 + count : 1 + 2 * count], refs[-1]
    k, v = side_by_side(ks), side_by_side(vs)
    for r in range(0, q_ref.shape[0], tile):
        sums = weigh(q_ref[r : r + tile, :], k, v, factor)
        if more:
            sums += refs[-2][r : r + tile, :]
        out_ref[r : r + tile, :] = sums


def key_specs(arrays, head, column):
    keys = [pl.BlockSpec((a.shape[0], a.shape[1] // 2, head), lambda h: (0, 0, column(h))) for a in arrays]
    values = [pl.BlockSpec((a.shape[0], a.shape[1] // 2, head), lambda h: (0, 1, column(h))) for a in arrays]
    return keys + values


def attend_part(proj, first, arrays, before=None):
    rows, head = proj.shape[0], proj.shape[1] // (2 * HEADS)
    heads = arrays[0].shape[2] // head
    keys = sum(a.shape[0] * a.shape[1] // 2 for a in arrays)
    sums = pl.BlockSpec((rows, head), lambda h: (0, h))
    more = before is not None
    return pl.pallas_call(
        functools.partial(partial_kernel, count=len(arrays), factor=float(head) ** -0.5, tile=256, more=more),
        grid=(heads,),
        in_specs=[pl.BlockSpec((rows, head), lambda h: (0, HEADS + first + h))]
        + key_specs(arrays, head, lambda h: h)
        + [sums] * more,
        out_specs=sums,
        out_shape=jax.ShapeDtypeStruct((rows, heads * head), jnp.float32),
        compiler_params=params(),
        cost_estimate=pl.CostEstimate(
            flops=8 * rows * keys * heads * head, bytes_accessed=4 * 2**20, transcendentals=rows * keys * heads
        ),
    )(proj, *arrays, *arrays, *([before] if more else []))


def finish_kernel(*refs, count, factor, tile):
    q_ref, ks, vs = refs[0], refs[1 : 1 + count], refs[1 + count : 1 + 2 * count]
    sums_ref, done_ref, proj_ref, base_ref, ws_ref, scale_ref, live_ref = refs[1 + 2 * count : 8 + 2 * count]
    gated_ref, score_ref, attn, done, gate, gated, into, back = refs[8 + 2 * count :]
    h = pl.program_id(0)
    rows, width = gated.shape
    reads = [
        pltpu.make_async_copy(done_ref, done, into.at[0]),
        pltpu.make_async_copy(proj_ref.at[:, pl.ds(0, width)], gate, into.at[1]),
    ]

    @pl.when(h == 0)
    def _():
        for read in reads:
            read.start()

    k, v = side_by_side(ks), side_by_side(vs)
    for r in range(0, rows, tile):
        attn[h, r : r + tile, :] = weigh(q_ref[r : r + tile, :], k, v, factor) + sums_ref[r : r + tile, :]

    @pl.when(h == pl.num_programs(0) - 1)
    def _():
        for read in reads:
            read.wait()
        writes = []
        for i, r in enumerate(range(0, rows, tile)):
            heads = [attn[j, r : r + tile, :] for j in range(attn.shape[0])] + [done[r : r + tile, :]]
            whole = jnp.concatenate(heads, axis=1) * scale_ref[0]
            part = (layer_norm(whole) * gate[r : r + tile, :].astype(jnp.float32)).astype(jnp.bfloat16)
            gated[r : r + tile, :] = part
            write = pltpu.make_async_copy(gated.at[pl.ds(r, tile)], gated_ref.at[pl.ds(r, tile)], back.at[i])
            write.start()
            writes.append(write)
            score = jnp.sum(part.astype(jnp.float32) * ws_ref[...], axis=-1).reshape(1, -1) + base_ref[i]
            slots = r + lax.broadcasted_iota(jnp.int32, (1, tile), 1)
            score = jnp.where(slots < live_ref[0], score, 0.0)
            score_ref[:, :, r : r + tile] = jnp.broadcast_to(score[None], (score_ref.shape[0], 1, tile))
        for write in writes:
            write.wait()


def finish(proj, arrays, sums, done, base, ws, scale, live, parts):
    rows, width = proj.shape[0], proj.shape[1] // 2
    head = width // HEADS
    left = arrays[0].shape[2] // head
    tile = base.shape[2]
    smem = pl.BlockSpec(memory_space=pltpu.SMEM)
    return pl.pallas_call(
        functools.partial(finish_kernel, count=len(arrays), factor=float(head) ** -0.5, tile=tile),
        grid=(left,),
        in_specs=[pl.BlockSpec((rows, head), lambda h: (0, HEADS + h))]
        + key_specs(arrays, head, lambda h: h)
        + [
            pl.BlockSpec((rows, head), lambda h: (0, h)),
            pl.BlockSpec(memory_space=pl.ANY),
            pl.BlockSpec(memory_space=pl.ANY),
            pl.BlockSpec(base.shape, lambda h: (0, 0, 0)),
            pl.BlockSpec((1, width), lambda h: (0, 0)),
            smem,
            smem,
        ],
        out_specs=[pl.BlockSpec(memory_space=pltpu.HBM), pl.BlockSpec((parts, 1, rows), lambda h: (0, 0, 0))],
        out_shape=[
            jax.ShapeDtypeStruct((rows, width), jnp.bfloat16),
            jax.ShapeDtypeStruct((parts, 1, rows), jnp.float32),
        ],
        scratch_shapes=[
            pltpu.VMEM((left, rows, head), jnp.float32),
            pltpu.VMEM(done.shape, jnp.float32),
            pltpu.VMEM((rows, width), jnp.bfloat16),
            pltpu.VMEM((rows, width), jnp.bfloat16),
            pltpu.SemaphoreType.DMA((2,)),
            pltpu.SemaphoreType.DMA((rows // tile,)),
        ],
        compiler_params=params(VMEM_MOST),
        cost_estimate=pl.CostEstimate(flops=2**32, bytes_accessed=12 * 2**20, transcendentals=2**22),
    )(proj, *arrays, *arrays, sums, done, proj, base, ws, scale, live)


def out_kernel(gated_ref, w_ref, tokens_ref, out_ref):
    y = tokens_ref[...].astype(jnp.float32) + jnp.dot(gated_ref[...], w_ref[...], preferred_element_type=jnp.float32)
    out_ref[...] = y.astype(jnp.bfloat16)


def project_out(gated, w_out, tokens, tile=256):
    rows, width = tokens.shape
    return pl.pallas_call(
        out_kernel,
        grid=(rows // tile,),
        in_specs=[
            pl.BlockSpec((tile, width), lambda i: (i, 0)),
            pl.BlockSpec((width, width), lambda i: (0, 0)),
            pl.BlockSpec((tile, width), lambda i: (i, 0)),
        ],
        out_specs=pl.BlockSpec((tile, width), lambda i: (i, 0)),
        out_shape=jax.ShapeDtypeStruct((rows, width), jnp.bfloat16),
        compiler_params=params(VMEM_MOST),
        cost_estimate=pl.CostEstimate(flops=2 * rows * width * width, bytes_accessed=7 * 2**20, transcendentals=0),
    )(gated, w_out, tokens)


def pick_kernel(index_ref, table_ref, out_ref):
    index = index_ref[...]
    count = index.shape[0]
    height, lanes = table_ref.shape
    onehot = (lax.broadcasted_iota(jnp.int32, (count, height), 1) == index // lanes).astype(jnp.bfloat16)
    rest = table_ref[...]
    rows = jnp.zeros((count, lanes), jnp.float32)
    for _ in range(3):
        part = rest.astype(jnp.bfloat16)
        rows += jnp.dot(onehot, part, preferred_element_type=jnp.float32)
        rest = rest - part.astype(jnp.float32)
    mine = lax.broadcasted_iota(jnp.int32, (count, lanes), 1) == index % lanes
    out_ref[...] = jnp.sum(jnp.where(mine, rows, 0.0), axis=-1).reshape(1, -1)


def pick(index, table):
    count = index.shape[0]
    return pl.pallas_call(
        pick_kernel,
        out_shape=jax.ShapeDtypeStruct((1, count), jnp.float32),
        compiler_params=params(),
    )(index.reshape(count, 1), table.reshape(-1, 128))


HEADS_A = 5
tie = lax.optimization_barrier


def shift(block, axis, step):
    return lax.ppermute(block, axis, shifted(lax.axis_size(axis), step))


def on_device(
    cand_tokens, hist_keys, hist_values, hist_len, cand_count, impressions, w_proj, w_out, score_w
):
    tokens = cand_tokens[0]
    rows, width = tokens.shape
    own = hist_keys.shape[1]
    head = width // HEADS
    cand = lax.axis_index(("z", "x"))
    core = lax.axis_index("core")
    many_y, many_core = lax.axis_size("y"), lax.axis_size("core")
    parts, many_z, many_x = lax.axis_size(("z", "x")), lax.axis_size("z"), lax.axis_size("x")

    mine_a, mine_b = stage(hist_len - cand * own, hist_keys[0], hist_values[0], HEADS_A * head, many_z)

    xs = [mine_a, shift(mine_a, "x", 1), shift(mine_a, "x", -1), shift(mine_a, "x", 2)]
    zs = lax.all_to_all(mine_b, "z", split_axis=0, concat_axis=0, tiled=True)
    w_near = [w_proj, shift(w_proj, "y", 1), shift(w_proj, "y", -1)]
    w_far, xs, w_near = tie((w_proj, xs, w_near))
    w_far = shift(w_far, "y", 2)
    swap = [(0, 1), (1, 0)]
    w_near = copies(1, *w_near)[0]
    w_other = lax.ppermute(w_near, "core", swap)
    normed, ws, base = prepare(tokens, w_out, score_w[None, :])

    p = q = start = copies(1, *xs)[0]
    zs = copies(many_x, zs)[:, 0]
    p, q, w_far, normed, w_other, _ = tie((shift(p, "z", 1), shift(q, "z", -1), w_far, normed, w_other, zs))
    b = lax.all_to_all(zs, "x", split_axis=0, concat_axis=0, tiled=True)
    b = b.reshape(-1, *mine_b.shape[1:])
    w_far_other = lax.ppermute(w_far, "core", swap)
    near = [start, p, q]
    p, q = shift(p, "z", 1), shift(q, "z", -1)
    block = (lax.axis_index("y") - jnp.array([0, 1, -1, 2])) % many_y * many_core
    mine, other = (block + core).astype(jnp.int32), (block + 1 - core).astype(jnp.int32)
    proj = project(normed, w_near, w_other, jnp.concatenate([mine[:3], other[:3]]), 2 * width)
    proj = project(normed, w_far[None], w_far_other[None], jnp.concatenate([mine[3:], other[3:]]), 2 * width, proj)
    p, q, proj = tie((p, q, proj))
    near += [p, q]
    p, q = shift(p, "z", 1), shift(q, "z", -1)
    sums = attend_part(proj, 0, near)
    p, q, sums = tie((p, q, sums))
    ring = [(c * many_z + i, c * many_z + (i + (1, -1)[c]) % many_z) for c in range(2) for i in range(many_z)]
    far = [p, q, lax.ppermute(jnp.where(core == 0, p, q), ("core", "z"), ring)]
    done = attend_part(proj, HEADS_A, [b])

    scale = 0.5 * float(head) ** -0.5 / hist_len.astype(jnp.float32)
    live = cand_count - cand * rows
    gated, sent = finish(proj, far, sums, done, base, ws, scale, live, parts)
    every = lax.all_to_all(sent, ("z", "x"), split_axis=0, concat_axis=0, tiled=True)
    layer_out = project_out(gated, w_out, tokens)
    ranked = pick(impressions[0], every)
    return (layer_out[None], ranked)


def solution(mesh):
    split = Mesh(mesh.devices.reshape(4, 2, 8, 4), ("y", "core", "z", "x"))
    users, cands = ("y", "core"), ("z", "x")
    return jax.shard_map(
        on_device,
        mesh=split,
        in_specs=(
            P(users, cands, None),
            P(users, cands, None),
            P(users, cands, None),
            P(users),
            P(users),
            P(users, cands),
            P(None, users),
            P(),
            P(),
        ),
        out_specs=(P(users, cands, None), P(users, cands)),
        check_vma=False,
    )
```

```python
import functools

import jax
import jax.numpy as jnp
from jax import lax
from jax.experimental import pallas as pl
from jax.experimental.pallas import tpu as pltpu
from jax.sharding import Mesh
from jax.sharding import PartitionSpec as P

HEADS = 8
eps = 1e-05
VMEM_LIMIT = 24 * 2**20
VMEM_MOST = 58 * 2**20


def params(limit=VMEM_LIMIT):
    return pltpu.CompilerParams(vmem_limit_bytes=limit)


def layer_norm(values):
    mean = jnp.mean(values, axis=-1, keepdims=True)
    centered = values - mean
    var = jnp.mean(centered * centered, axis=-1, keepdims=True)
    return centered * lax.rsqrt(var + eps)


def shifted(size, step):
    return [(i, (i + step) % size) for i in range(size)]


def prepare_kernel(tokens_ref, w_ref, sw_ref, normed_ref, ws_ref, base_ref):
    tokens = tokens_ref[...].astype(jnp.float32)
    normed_ref[...] = layer_norm(tokens).astype(jnp.bfloat16)
    base_ref[...] = jnp.sum(tokens * sw_ref[...], axis=-1).reshape(1, 1, -1)

    @pl.when(pl.program_id(0) == 0)
    def _():
        ws_ref[...] = lax.dot_general(
            sw_ref[...],
            w_ref[...].astype(jnp.float32),
            (((1,), (1,)), ((), ())),
            precision=lax.Precision.HIGHEST,
            preferred_element_type=jnp.float32,
        )


def prepare(tokens, w_out, score_w, steps=3):
    rows, width = tokens.shape
    tile, part = rows // steps, width
    return pl.pallas_call(
        prepare_kernel,
        grid=(steps,),
        in_specs=[
            pl.BlockSpec((tile, width), lambda i: (i, 0)),
            pl.BlockSpec((part, width), lambda i: (0, 0)),
            pl.BlockSpec((1, width), lambda i: (0, 0)),
        ],
        out_specs=[
            pl.BlockSpec((tile, width), lambda i: (i, 0)),
            pl.BlockSpec((1, part), lambda i: (0, 0)),
            pl.BlockSpec((1, 1, tile), lambda i: (i, 0, 0)),
        ],
        out_shape=[
            jax.ShapeDtypeStruct((rows, width), jnp.bfloat16),
            jax.ShapeDtypeStruct((1, width), jnp.float32),
            jax.ShapeDtypeStruct((steps, 1, tile), jnp.float32),
        ],
        compiler_params=params(),
        cost_estimate=pl.CostEstimate(flops=2**27, bytes_accessed=6 * 2**20, transcendentals=rows),
    )(tokens, w_out, score_w)


def project_kernel(place_ref, normed_ref, first_ref, second_ref, *rest, count):
    w = jnp.where(pl.program_id(0) < count, first_ref[0], second_ref[0])
    x = 0.5 * jnp.dot(normed_ref[...], w, preferred_element_type=jnp.float32)
    rest[-1][...] = (x + x * jnp.tanh(x)).astype(jnp.bfloat16)


def project(normed, first, second, place, total, into=None):
    rows, width = normed.shape
    count, _, columns = first.shape
    many = count + second.shape[0]
    more = into is not None
    return pl.pallas_call(
        functools.partial(project_kernel, count=count),
        grid_spec=pltpu.PrefetchScalarGridSpec(
            num_scalar_prefetch=1,
            grid=(many,),
            in_specs=[
                pl.BlockSpec((rows, width), lambda j, o: (0, 0)),
                pl.BlockSpec((1, width, columns), lambda j, o: (jnp.minimum(j, count - 1), 0, 0)),
                pl.BlockSpec((1, width, columns), lambda j, o: (jnp.maximum(j - count, 0), 0, 0)),
            ]
            + [pl.BlockSpec(memory_space=pl.ANY)] * more,
            out_specs=pl.BlockSpec((rows, columns), lambda j, o: (0, o[j])),
        ),
        out_shape=jax.ShapeDtypeStruct((rows, total), jnp.bfloat16),
        input_output_aliases={4: 0} if more else {},
        compiler_params=params(),
        cost_estimate=pl.CostEstimate(
            flops=2 * rows * width * many * columns, bytes_accessed=5 * 2**20, transcendentals=rows * many * columns
        ),
    )(place, normed, first, second, *([into] if more else []))


def copies_kernel(*refs):
    ins, out, held, into, back = refs[:-4], refs[-4], refs[-3], refs[-2], refs[-1]
    reads = [pltpu.make_async_copy(ref, held.at[j], into.at[j]) for j, ref in enumerate(ins)]
    for read in reads:
        read.start()
    writes = []
    for j, read in enumerate(reads):
        read.wait()
        for i in range(out.shape[0]):
            write = pltpu.make_async_copy(held.at[j], out.at[i, j], back.at[i, j])
            write.start()
            writes.append(write)
    for write in writes:
        write.wait()


def copies(times, *blocks):
    held = (len(blocks),) + blocks[0].shape
    return pl.pallas_call(
        copies_kernel,
        in_specs=[pl.BlockSpec(memory_space=pl.ANY)] * len(blocks),
        out_specs=pl.BlockSpec(memory_space=pl.ANY),
        out_shape=jax.ShapeDtypeStruct((times,) + held, blocks[0].dtype),
        scratch_shapes=[
            pltpu.VMEM(held, blocks[0].dtype),
            pltpu.SemaphoreType.DMA((len(blocks),)),
            pltpu.SemaphoreType.DMA((times, len(blocks))),
        ],
        compiler_params=params(),
        cost_estimate=pl.CostEstimate(flops=0, bytes_accessed=2**22, transcendentals=0),
    )(*blocks)


def stage_kernel(live_ref, keys_ref, values_ref, a_ref, b_ref, *, cut):
    own = keys_ref.shape[0]
    valid = lax.broadcasted_iota(jnp.int32, keys_ref.shape, 0) < live_ref[0]
    keys = jnp.where(valid, keys_ref[...], jnp.zeros((), keys_ref.dtype))
    values = values_ref[...]
    a_ref[:own], a_ref[own:] = keys[:, :cut], values[:, :cut]
    for i in range(b_ref.shape[0]):
        b_ref[i, :own], b_ref[i, own:] = keys[:, cut:], values[:, cut:]


def stage(live, keys, values, cut, times):
    own, width = keys.shape
    return pl.pallas_call(
        functools.partial(stage_kernel, cut=cut),
        in_specs=[
            pl.BlockSpec(memory_space=pltpu.SMEM),
            pl.BlockSpec(memory_space=pltpu.VMEM),
            pl.BlockSpec(memory_space=pltpu.VMEM),
        ],
        out_shape=[
            jax.ShapeDtypeStruct((2 * own, cut), keys.dtype),
            jax.ShapeDtypeStruct((times, 2 * own, width - cut), keys.dtype),
        ],
        compiler_params=params(VMEM_MOST),
    )(live, keys, values)


def side_by_side(refs):
    blocks = [ref[...].reshape(-1, ref.shape[-1]) for ref in refs]
    return jnp.concatenate(blocks, axis=0) if len(blocks) > 1 else blocks[0]


def weigh(q, k, v, factor):
    s = lax.dot_general(q, k, (((1,), (1,)), ((), ())), preferred_element_type=jnp.float32)
    w = (s * jnp.tanh(s * (0.5 * factor)) + s).astype(jnp.bfloat16)
    return jnp.dot(w, v, preferred_element_type=jnp.float32)


def partial_kernel(*refs, count, factor, tile, more):
    q_ref, ks, vs, out_ref = refs[0], refs[1 : 1 + count], refs[1 + count : 1 + 2 * count], refs[-1]
    k, v = side_by_side(ks), side_by_side(vs)
    for r in range(0, q_ref.shape[0], tile):
        sums = weigh(q_ref[r : r + tile, :], k, v, factor)
        if more:
            sums += refs[-2][r : r + tile, :]
        out_ref[r : r + tile, :] = sums


def key_specs(arrays, head, column):
    keys = [pl.BlockSpec((a.shape[0], a.shape[1] // 2, head), lambda h: (0, 0, column(h))) for a in arrays]
    values = [pl.BlockSpec((a.shape[0], a.shape[1] // 2, head), lambda h: (0, 1, column(h))) for a in arrays]
    return keys + values


def attend_part(proj, first, arrays, before=None):
    rows, head = proj.shape[0], proj.shape[1] // (2 * HEADS)
    heads = arrays[0].shape[2] // head
    keys = sum(a.shape[0] * a.shape[1] // 2 for a in arrays)
    sums = pl.BlockSpec((rows, head), lambda h: (0, h))
    more = before is not None
    return pl.pallas_call(
        functools.partial(partial_kernel, count=len(arrays), factor=float(head) ** -0.5, tile=rows, more=more),
        grid=(heads,),
        in_specs=[pl.BlockSpec((rows, head), lambda h: (0, HEADS + first + h))]
        + key_specs(arrays, head, lambda h: h)
        + [sums] * more,
        out_specs=sums,
        out_shape=jax.ShapeDtypeStruct((rows, heads * head), jnp.float32),
        compiler_params=params(),
        cost_estimate=pl.CostEstimate(
            flops=8 * rows * keys * heads * head, bytes_accessed=4 * 2**20, transcendentals=rows * keys * heads
        ),
    )(proj, *arrays, *arrays, *([before] if more else []))


def finish_kernel(*refs, count, factor, tile):
    q_ref, ks, vs = refs[0], refs[1 : 1 + count], refs[1 + count : 1 + 2 * count]
    sums_ref, done_ref, proj_ref, base_ref, ws_ref, scale_ref, live_ref = refs[1 + 2 * count : 8 + 2 * count]
    gated_ref, score_ref, attn, done, gate, gated, into, back = refs[8 + 2 * count :]
    h = pl.program_id(0)
    rows, width = gated.shape
    reads = [
        pltpu.make_async_copy(done_ref, done, into.at[0]),
        pltpu.make_async_copy(proj_ref.at[:, pl.ds(0, width)], gate, into.at[1]),
    ]

    @pl.when(h == 0)
    def _():
        for read in reads:
            read.start()

    k, v = side_by_side(ks), side_by_side(vs)
    attn[h] = weigh(q_ref[...], k, v, factor) + sums_ref[...]

    @pl.when(h == pl.num_programs(0) - 1)
    def _():
        for read in reads:
            read.wait()
        writes = []
        for i, r in enumerate(range(0, rows, tile)):
            heads = [attn[j, r : r + tile, :] for j in range(attn.shape[0])] + [done[r : r + tile, :]]
            whole = jnp.concatenate(heads, axis=1) * scale_ref[0]
            part = (layer_norm(whole) * gate[r : r + tile, :].astype(jnp.float32)).astype(jnp.bfloat16)
            gated[r : r + tile, :] = part
            write = pltpu.make_async_copy(gated.at[pl.ds(r, tile)], gated_ref.at[pl.ds(r, tile)], back.at[i])
            write.start()
            writes.append(write)
            score = jnp.sum(part.astype(jnp.float32) * ws_ref[...], axis=-1).reshape(1, -1) + base_ref[i]
            slots = r + lax.broadcasted_iota(jnp.int32, (1, tile), 1)
            score = jnp.where(slots < live_ref[0], score, 0.0)
            score_ref[:, :, r : r + tile] = jnp.broadcast_to(score[None], (score_ref.shape[0], 1, tile))
        for write in writes:
            write.wait()


def finish(proj, arrays, sums, done, base, ws, scale, live, parts):
    rows, width = proj.shape[0], proj.shape[1] // 2
    head = width // HEADS
    left = arrays[0].shape[2] // head
    tile = base.shape[2]
    smem = pl.BlockSpec(memory_space=pltpu.SMEM)
    return pl.pallas_call(
        functools.partial(finish_kernel, count=len(arrays), factor=float(head) ** -0.5, tile=tile),
        grid=(left,),
        in_specs=[pl.BlockSpec((rows, head), lambda h: (0, HEADS + h))]
        + key_specs(arrays, head, lambda h: h)
        + [
            pl.BlockSpec((rows, head), lambda h: (0, h)),
            pl.BlockSpec(memory_space=pl.ANY),
            pl.BlockSpec(memory_space=pl.ANY),
            pl.BlockSpec(base.shape, lambda h: (0, 0, 0)),
            pl.BlockSpec((1, width), lambda h: (0, 0)),
            smem,
            smem,
        ],
        out_specs=[pl.BlockSpec(memory_space=pltpu.HBM), pl.BlockSpec((parts, 1, rows), lambda h: (0, 0, 0))],
        out_shape=[
            jax.ShapeDtypeStruct((rows, width), jnp.bfloat16),
            jax.ShapeDtypeStruct((parts, 1, rows), jnp.float32),
        ],
        scratch_shapes=[
            pltpu.VMEM((left, rows, head), jnp.float32),
            pltpu.VMEM(done.shape, jnp.float32),
            pltpu.VMEM((rows, width), jnp.bfloat16),
            pltpu.VMEM((rows, width), jnp.bfloat16),
            pltpu.SemaphoreType.DMA((2,)),
            pltpu.SemaphoreType.DMA((rows // tile,)),
        ],
        compiler_params=params(VMEM_MOST),
        cost_estimate=pl.CostEstimate(flops=2**32, bytes_accessed=12 * 2**20, transcendentals=2**22),
    )(proj, *arrays, *arrays, sums, done, proj, base, ws, scale, live)


def out_kernel(gated_ref, w_ref, tokens_ref, out_ref):
    y = tokens_ref[...].astype(jnp.float32) + jnp.dot(gated_ref[...], w_ref[...], preferred_element_type=jnp.float32)
    out_ref[...] = y.astype(jnp.bfloat16)


def project_out(gated, w_out, tokens, tile=256):
    rows, width = tokens.shape
    return pl.pallas_call(
        out_kernel,
        grid=(rows // tile,),
        in_specs=[
            pl.BlockSpec((tile, width), lambda i: (i, 0)),
            pl.BlockSpec((width, width), lambda i: (0, 0)),
            pl.BlockSpec((tile, width), lambda i: (i, 0)),
        ],
        out_specs=pl.BlockSpec((tile, width), lambda i: (i, 0)),
        out_shape=jax.ShapeDtypeStruct((rows, width), jnp.bfloat16),
        compiler_params=params(VMEM_MOST),
        cost_estimate=pl.CostEstimate(flops=2 * rows * width * width, bytes_accessed=7 * 2**20, transcendentals=0),
    )(gated, w_out, tokens)


def pick_kernel(index_ref, table_ref, out_ref):
    index = index_ref[...]
    count = index.shape[0]
    height, lanes = table_ref.shape
    onehot = (lax.broadcasted_iota(jnp.int32, (count, height), 1) == index // lanes).astype(jnp.bfloat16)
    rest = table_ref[...]
    rows = jnp.zeros((count, lanes), jnp.float32)
    for _ in range(3):
        part = rest.astype(jnp.bfloat16)
        rows += jnp.dot(onehot, part, preferred_element_type=jnp.float32)
        rest = rest - part.astype(jnp.float32)
    mine = lax.broadcasted_iota(jnp.int32, (count, lanes), 1) == index % lanes
    out_ref[...] = jnp.sum(jnp.where(mine, rows, 0.0), axis=-1).reshape(1, -1)


def pick(index, table):
    count = index.shape[0]
    return pl.pallas_call(
        pick_kernel,
        out_shape=jax.ShapeDtypeStruct((1, count), jnp.float32),
        compiler_params=params(),
    )(index.reshape(count, 1), table.reshape(-1, 128))


HEADS_A = 5
tie = lax.optimization_barrier


def shift(block, axis, step):
    return lax.ppermute(block, axis, shifted(lax.axis_size(axis), step))


def on_device(
    cand_tokens, hist_keys, hist_values, hist_len, cand_count, impressions, w_proj, w_out, score_w
):
    tokens = cand_tokens[0]
    rows, width = tokens.shape
    own = hist_keys.shape[1]
    head = width // HEADS
    cand = lax.axis_index(("z", "x"))
    core = lax.axis_index("core")
    many_y, many_core = lax.axis_size("y"), lax.axis_size("core")
    parts, many_z, many_x = lax.axis_size(("z", "x")), lax.axis_size("z"), lax.axis_size("x")

    mine_a, mine_b = stage(hist_len - cand * own, hist_keys[0], hist_values[0], HEADS_A * head, many_z)

    xs = [mine_a, shift(mine_a, "x", 1), shift(mine_a, "x", -1), shift(mine_a, "x", 2)]
    zs = lax.all_to_all(mine_b, "z", split_axis=0, concat_axis=0, tiled=True)
    w_near = [w_proj, shift(w_proj, "y", 1), shift(w_proj, "y", -1)]
    w_far, xs, w_near = tie((w_proj, xs, w_near))
    w_far = shift(w_far, "y", 2)
    swap = [(0, 1), (1, 0)]
    w_near = copies(1, *w_near)[0]
    w_other = lax.ppermute(w_near, "core", swap)
    normed, ws, base = prepare(tokens, w_out, score_w[None, :])

    p = q = start = copies(1, *xs)[0]
    zs = copies(many_x, zs)[:, 0]
    p, q, w_far, normed, w_other, _ = tie((shift(p, "z", 1), shift(q, "z", -1), w_far, normed, w_other, zs))
    b = lax.all_to_all(zs, "x", split_axis=0, concat_axis=0, tiled=True)
    b = b.reshape(-1, *mine_b.shape[1:])
    w_far_other = lax.ppermute(w_far, "core", swap)
    near = [start, p, q]
    p, q = shift(p, "z", 1), shift(q, "z", -1)
    block = (lax.axis_index("y") - jnp.array([0, 1, -1, 2])) % many_y * many_core
    mine, other = (block + core).astype(jnp.int32), (block + 1 - core).astype(jnp.int32)
    proj = project(normed, w_near, w_other, jnp.concatenate([mine[:3], other[:3]]), 2 * width)
    proj = project(normed, w_far[None], w_far_other[None], jnp.concatenate([mine[3:], other[3:]]), 2 * width, proj)
    p, q, proj = tie((p, q, proj))
    near += [p, q]
    p, q = shift(p, "z", 1), shift(q, "z", -1)
    sums = attend_part(proj, 0, near)
    p, q, sums = tie((p, q, sums))
    ring = [(c * many_z + i, c * many_z + (i + (1, -1)[c]) % many_z) for c in range(2) for i in range(many_z)]
    far = [p, q, lax.ppermute(jnp.where(core == 0, p, q), ("core", "z"), ring)]
    done = attend_part(proj, HEADS_A, [b])

    scale = 0.5 * float(head) ** -0.5 / hist_len.astype(jnp.float32)
    live = cand_count - cand * rows
    gated, sent = finish(proj, far, sums, done, base, ws, scale, live, parts)
    every = lax.all_to_all(sent, ("z", "x"), split_axis=0, concat_axis=0, tiled=True)
    layer_out = project_out(gated, w_out, tokens)
    ranked = pick(impressions[0], every)
    return (layer_out[None], ranked)


def solution(mesh):
    split = Mesh(mesh.devices.reshape(4, 2, 8, 4), ("y", "core", "z", "x"))
    users, cands = ("y", "core"), ("z", "x")
    return jax.shard_map(
        on_device,
        mesh=split,
        in_specs=(
            P(users, cands, None),
            P(users, cands, None),
            P(users, cands, None),
            P(users),
            P(users),
            P(users, cands),
            P(None, users),
            P(),
            P(),
        ),
        out_specs=(P(users, cands, None), P(users, cands)),
        check_vma=False,
    )
```
